256 devices in a mesh: wide: 32 (over y, z_hi, core), narrow: 8 (over x, z_lo).
Axes of the slice: x: 4, y: 4, z: 8 (z_hi: 4, z_lo: 2; z = z_hi * 2 + z_lo), core: 2. Of those that a mesh axis runs over, the one named last changes fastest.
Arguments:
- a_hamiltonian: bfloat16 [8, 32, 72, 9216], P('narrow', 'wide'), may hold values from -0.875 to 0.875
- a_margin: bfloat16 [8, 32, 72, 9216], P('narrow', 'wide'), may hold values from -0.625 to 0.625
- a_slots: int32 [8, 32, 2, 72], P('narrow', 'wide'), may hold values from 0 to 11, as said below
- a_count: int32 [8, 32], P('narrow', 'wide'), may hold values from 36 to 72, as said below
- a_molecules: int32 [8, 32, 2, 12, 16], P('narrow', 'wide'), may hold values from 0 to 393215
- b_hamiltonian: bfloat16 [8, 32, 72, 9216], P('narrow', 'wide'), may hold values from -0.875 to 0.875
- b_margin: bfloat16 [8, 32, 72, 9216], P('narrow', 'wide'), may hold values from -0.625 to 0.625
- b_slots: int32 [8, 32, 2, 72], P('narrow', 'wide'), may hold values from 0 to 11, as said below
- b_count: int32 [8, 32], P('narrow', 'wide'), may hold values from 36 to 72, as said below
- b_molecules: int32 [8, 32, 2, 12, 16], P('narrow', 'wide'), may hold values from 0 to 393215
- charge_shift: float32 [3, 393216], P(None, 'wide'), may hold values from -6 to 6
Outputs:
- product_tile: bfloat16 [8, 32, 1152, 1152], P('narrow', 'wide')
The draws below stay inside these ranges and needn't reach their ends.
Inputs may be any that keep to these rules, and one draw needn't show every extreme that they name: `a_slots`: entries are block numbers within a tile; the first a_count entries of a tile name distinct (row, column) pairs. `a_count`: some tile has all 72 slots occupied. `b_slots`: entries are block numbers within a tile; the first b_count entries of a tile name distinct (row, column) pairs. `b_count`: some tile has all 72 slots occupied.
All inputs are finite; a program needn't handle non-finite values.
Results may differ from the reference program's by a relative error of at most 0.0057.
Values may be sent and summed in bfloat16 or wider, within the bound.
A program may use at most 128 MiB of HBM per device.

```python
import jax
import jax.numpy as jnp
from jax import lax

TB = 12
MB = 16
BLK = 96
SLOTS = 72
MOLS = 393216
GRID_ROWS = 8
GRID_COLS = 32


def slot_lists(base):
    tile_count = GRID_ROWS * GRID_COLS
    subkeys = jax.random.split(base, tile_count)

    def shuffle_one(subkey):
        return jax.random.permutation(subkey, TB * TB)
    shuffled = jax.vmap(shuffle_one)(subkeys)[:, :SLOTS].astype(jnp.int32)
    row_part = shuffled // TB
    col_part = shuffled % TB
    return jnp.stack([row_part, col_part], axis=1).reshape(GRID_ROWS, GRID_COLS, 2, SLOTS).astype(jnp.int32)


def count_lists(base):
    tile_count = GRID_ROWS * GRID_COLS
    level_key, spot_key = jax.random.split(base)
    counts = jax.random.randint(level_key, (tile_count,), SLOTS // 2, SLOTS + 1, dtype=jnp.int32)
    fullest = jax.random.randint(spot_key, (), 0, tile_count, dtype=jnp.int32)
    counts = jnp.where(jnp.arange(tile_count, dtype=jnp.int32) == fullest, SLOTS, counts)
    return counts.reshape(GRID_ROWS, GRID_COLS).astype(jnp.int32)


def draw_a_slots(key, part):
    key = jax.random.fold_in(key, 11)
    return slot_lists(key)


def draw_a_count(key, part):
    key = jax.random.fold_in(key, 12)
    return count_lists(key)


def draw_b_slots(key, part):
    key = jax.random.fold_in(key, 13)
    return slot_lists(key)


def draw_b_count(key, part):
    key = jax.random.fold_in(key, 14)
    return count_lists(key)


def place_ends(values, rng, least, high):
    longest = values.shape.index(max(values.shape))
    spots = []
    for shift in (0, 1):
        where = [jax.random.randint(jax.random.fold_in(rng, axis), (), 0, length) for axis, length in enumerate(values.shape)]
        where[longest] = (where[longest] + shift) % values.shape[longest]
        spots.append(tuple(where))
    return values.at[spots[0]].set(least).at[spots[1]].set(high)


def levels(rng, dims, shards, low, top_value):
    level, own = 1.0, jax.random.fold_in(rng, 6)
    for dim, shards_of in shards:
        steps = jnp.exp(jax.random.uniform(jax.random.fold_in(own, dim), (shards_of,), jnp.float32, low / len(shards), top_value / len(shards)))
        level = level * jnp.repeat(steps, dims[dim] // shards_of).reshape([-1 if axis == dim else 1 for axis in range(len(dims))])
    return level


def scatter_about(key, shape, deviation, reach, shards=(), kind=jnp.bfloat16):
    gain = levels(key, shape, shards, -0.22, 0.18) if shards else 1.0
    values = jax.random.normal(key, shape, jnp.float32) * deviation * gain
    return jnp.minimum(jnp.maximum(values, -reach), reach).astype(kind)


def setup_inputs(seed: int = 0) -> dict:
    key_list = jax.random.split(jax.random.key(seed), 12)
    a_hamiltonian = scatter_about(key_list[0], (GRID_ROWS, GRID_COLS, SLOTS, BLK * BLK), 0.15, 0.875, ((0, 8), (1, 32)))
    a_margin = scatter_about(key_list[1], (GRID_ROWS, GRID_COLS, SLOTS, BLK * BLK), 0.1, 0.625, ((0, 8), (1, 32)))
    a_slots = draw_a_slots(jax.random.fold_in(key_list[11], 71), 0)
    a_count = draw_a_count(jax.random.fold_in(key_list[11], 71), 0)
    a_molecules = place_ends(jax.random.randint(key_list[4], (GRID_ROWS, GRID_COLS, 2, TB, MB), 0, MOLS), jax.random.fold_in(key_list[4], 1), 0, MOLS - 1).astype(jnp.int32)
    b_hamiltonian = scatter_about(key_list[5], (GRID_ROWS, GRID_COLS, SLOTS, BLK * BLK), 0.15, 0.875, ((0, 8), (1, 32)))
    b_margin = scatter_about(key_list[6], (GRID_ROWS, GRID_COLS, SLOTS, BLK * BLK), 0.1, 0.625, ((0, 8), (1, 32)))
    b_slots = draw_b_slots(jax.random.fold_in(key_list[11], 71), 0)
    b_count = draw_b_count(jax.random.fold_in(key_list[11], 71), 0)
    b_molecules = place_ends(jax.random.randint(key_list[9], (GRID_ROWS, GRID_COLS, 2, TB, MB), 0, MOLS), jax.random.fold_in(key_list[9], 1), 0, MOLS - 1).astype(jnp.int32)
    charge_shift = scatter_about(key_list[10], (3, MOLS), 1.0, 6.0, ((1, 32),), jnp.float32)
    return dict(a_hamiltonian=a_hamiltonian, a_margin=a_margin, a_slots=a_slots, a_count=a_count, a_molecules=a_molecules, b_hamiltonian=b_hamiltonian, b_margin=b_margin, b_slots=b_slots, b_count=b_count, b_molecules=b_molecules, charge_shift=charge_shift)


chem_level = 0.3


def assemble_blocks(hamil_list, margin_list, slot_table, picked):
    orbitals = jnp.stack([picked[0], picked[0], picked[0], picked[0], picked[1], picked[2]], axis=-1)
    orbitals = orbitals.reshape(2, TB, BLK)
    row_shift = jnp.take(orbitals[0], slot_table[0], axis=0)
    col_shift = jnp.take(orbitals[1], slot_table[1], axis=0)
    row_spread = jnp.repeat(row_shift, BLK, axis=1)
    col_spread = jnp.tile(col_shift, (1, BLK))
    hamil_float = hamil_list.astype(jnp.float32)
    margin_float = margin_list.astype(jnp.float32)
    hamiltonian = hamil_float + 0.5 * margin_float * (row_spread + col_spread)
    initial_density = chem_level * margin_float - hamiltonian
    return initial_density.astype(jnp.bfloat16)


def densify_tile(block_list, slot_table, live_count):
    position = slot_table[0] * TB + slot_table[1]
    occupied = jnp.arange(block_list.shape[0], dtype=jnp.int32) < live_count
    targets = jnp.arange(TB * TB, dtype=jnp.int32)
    selector = ((targets[:, None] == position[None, :]) & occupied[None, :]).astype(block_list.dtype)
    scattered = jnp.dot(selector, block_list, preferred_element_type=jnp.float32).astype(jnp.bfloat16)
    return scattered.reshape(TB, TB, BLK, BLK).transpose(0, 2, 1, 3).reshape(TB * BLK, TB * BLK)


def build_tile(hamil_list, margin_list, slot_table, live_count, molecule_ids, shift_table):
    picked = jnp.take(shift_table, molecule_ids.reshape(-1), axis=1).reshape(3, 2, TB, MB)
    blocks = assemble_blocks(hamil_list, margin_list, slot_table, picked)
    return densify_tile(blocks, slot_table, live_count)


def reference(a_hamiltonian, a_margin, a_slots, a_count, a_molecules, b_hamiltonian, b_margin, b_slots, b_count, b_molecules, charge_shift):
    def left_at(grid_row, grid_col):
        return build_tile(a_hamiltonian[grid_row, grid_col], a_margin[grid_row, grid_col], a_slots[grid_row, grid_col], a_count[grid_row, grid_col], a_molecules[grid_row, grid_col], charge_shift)

    def right_at(grid_row, grid_col):
        return build_tile(b_hamiltonian[grid_row, grid_col], b_margin[grid_row, grid_col], b_slots[grid_row, grid_col], b_count[grid_row, grid_col], b_molecules[grid_row, grid_col], charge_shift)

    def tile_product(tile_number):
        grid_row = (tile_number // GRID_COLS).astype(jnp.int32)
        grid_col = (tile_number % GRID_COLS).astype(jnp.int32)
        next_col = ((grid_col + 1) % GRID_COLS).astype(jnp.int32)
        next_row = ((grid_row + 1) % GRID_ROWS).astype(jnp.int32)
        first_term = jnp.dot(left_at(grid_row, grid_col), right_at(grid_row, grid_col), preferred_element_type=jnp.float32)
        second_term = jnp.dot(left_at(grid_row, next_col), right_at(next_row, grid_col), preferred_element_type=jnp.float32)
        return (first_term + second_term).astype(jnp.bfloat16)

    flat = lax.map(tile_product, jnp.arange(GRID_ROWS * GRID_COLS, dtype=jnp.int32))
    return flat.reshape(GRID_ROWS, GRID_COLS, TB * BLK, TB * BLK)
```

```python
import functools

import jax
import jax.numpy as jnp
from jax import lax
from jax.experimental import pallas as pl
from jax.experimental.pallas import tpu as pltpu
from jax.sharding import PartitionSpec as P

TB = 12
MB = 16
BLK = 96
SLOTS = 72
FLAT = BLK * BLK
ROWS = 16
CHUNKS = BLK // ROWS
LANES = ROWS * BLK
PART = TB * ROWS
KPAD = TB * 128
SIDE = TB * BLK
CHIPS = 16
NW, NN = 32, 8
TABLE = 12288
CHEM = 0.3

MESH = pl.DeviceIdType.MESH
F32, BF16, I32 = jnp.float32, jnp.bfloat16, jnp.int32


def iota(shape, dim):
    return lax.broadcasted_iota(I32, shape, dim)


def kernel(
    a_h, a_m, a_slots, a_count, a_mol, b_h, b_m, b_slots, b_count, b_mol, table, out,
    h_l, m_l, h_r, m_r, blk_l, blk_r, got_l, got_r, right, first, rows_ir, rows_ri, done,
    sel, perm, pos, pos_got, ask, asked, reply, answer, table2, hi_s, lo_s, found, row_q, col_q,
    load_sem, out_sem, ask_s, ask_r, rep_s, rep_r, pos_s, pos_r, tab_s, tab_r,
    l_s, l_r, r_s, r_r,
):
    n, w = lax.axis_index("narrow"), lax.axis_index("wide")
    core, chip = lax.rem(w, 2), lax.div(w, 2)
    partner = w + 1 - 2 * core
    beyond = lax.rem(w - 1 + 2 * core + NW, NW)
    w_down = lax.rem(w + NW - 1, NW)
    n_down, n_up = lax.rem(n + NN - 1, NN), lax.rem(n + 1, NN)

    def dev(nn, ww):
        return {"narrow": nn, "wide": ww}

    def peer(i):
        return dev(n, 2 * lax.rem(chip + i, CHIPS) + core)

    loads = [
        pltpu.make_async_copy(src, dst, load_sem.at[k])
        for k, (src, dst) in enumerate([(b_h, h_r), (b_m, m_r), (a_h, h_l), (a_m, m_l)])
    ]
    for copy in loads:
        copy.start()

    barrier = pltpu.get_barrier_semaphore()
    known = [peer(i) for i in range(1, CHIPS)]
    known += [dev(n, partner), dev(n, beyond), dev(n_down, w), dev(n_up, w)]
    for device in known:
        pl.semaphore_signal(barrier, inc=1, device_id=device, device_id_type=MESH)

    mols = jnp.concatenate([a_mol[0], a_mol[1], b_mol[0], b_mol[1]], axis=1)
    folded = jnp.concatenate([mols[0:6], mols[6:12]], axis=1)
    ask[0:6, :] = folded
    ask[6:8, :] = jnp.zeros((2, 128), I32)
    asked[0, 0:6, :] = folded
    for f, (slots, count) in enumerate([(a_slots, a_count), (b_slots, b_count)]):
        place = slots[1:2, :] * (2 * TB) + slots[0:1, :]
        live = iota((1, SLOTS), 1) < count[0:1, 0:1]
        pos[f] = jnp.full((8, 128), -1, I32)
        pos[f, 0:1, 0:SLOTS] = jnp.where(live, place, -1)

    pl.semaphore_wait(barrier, len(known))

    def remote(src, dst, s, r, device):
        return pltpu.make_async_remote_copy(
            src_ref=src, dst_ref=dst, send_sem=s, recv_sem=r, device_id=device, device_id_type=MESH
        )

    asks = [remote(ask, asked.at[CHIPS - i], ask_s.at[i], ask_r.at[CHIPS - i], peer(i)) for i in range(1, CHIPS)]
    for copy in asks:
        copy.start()
    tab_copy = remote(table, table2, tab_s, tab_r, dev(n, partner))
    tab_copy.start()
    pos_copies = [
        remote(pos.at[0], pos_got.at[0], pos_s.at[0], pos_r.at[0], dev(n, w_down)),
        remote(pos.at[1], pos_got.at[1], pos_s.at[1], pos_r.at[1], dev(n_down, w)),
    ]
    for copy in pos_copies:
        copy.start()

    def selection(k, place):
        wide = jnp.concatenate([place, jnp.where(place < 0, -1, place + TB)], axis=1)
        hit = iota((2 * TB * TB, 2 * SLOTS), 0) == wide
        sel[k] = jnp.where(hit, 1.0, 0.0).astype(BF16)

    selection(0, pos[0, 0:1, 0:SLOTS])
    selection(1, pos[1, 0:1, 0:SLOTS])
    pr, pc = iota((PART, PART), 0), iota((PART, PART), 1)
    perm[...] = jnp.where(pc == (pr % ROWS) * TB + pr // ROWS, 1.0, 0.0).astype(BF16)
    for k in range(2):
        for t in range(TB):
            right[k, t * 128 + BLK : (t + 1) * 128, :] = jnp.zeros((128 - BLK, SIDE), BF16)

    for copy in asks:
        copy.wait_recv()
    for i in range(CHIPS):
        local = asked[i, 0:6, :] - chip * (2 * TABLE)
        hi_s[6 * i : 6 * i + 6, :] = local >> 7
        lo_s[6 * i : 6 * i + 6, :] = local & 127
    found[...] = jnp.zeros_like(found)
    tab_copy.wait_recv()

    def search(tab, base):
        def group(v, _):
            at = pl.ds(pl.multiple_of(v * 24, 8), 24)
            hi, lo = hi_s[at, :] - base, lo_s[at, :]

            def step(h, acc):
                lanes = pl.ds(pl.multiple_of(h * 128, 128), 128)
                hit = hi == h
                new = []
                for q in range(3):
                    line = jnp.broadcast_to(tab[q : q + 1, lanes], (24, 128))
                    value = jnp.take_along_axis(line, lo, axis=1)
                    new.append(jnp.where(hit, value, acc[q]))
                return tuple(new)

            acc = lax.fori_loop(0, TABLE // 128, step, tuple(found[q, at, :] for q in range(3)), unroll=4)
            for q in range(3):
                found[q, at, :] = acc[q]
            return 0

        lax.fori_loop(0, 4, group, 0)

    search(table, core * (TABLE // 128))
    search(table2, (1 - core) * (TABLE // 128))

    for i in range(CHIPS):
        for q in range(3):
            reply[i, 6 * q : 6 * q + 6, :] = found[q, 6 * i : 6 * i + 6, :]
    replies = [
        remote(reply.at[i], answer.at[CHIPS - i], rep_s.at[i], rep_r.at[CHIPS - i], peer(i)) for i in range(1, CHIPS)
    ]
    for copy in replies:
        copy.start()
    for copy in replies:
        copy.wait_recv()
    total = reply[0]
    for i in range(1, CHIPS):
        total += answer[i]

    charge = []
    for q in range(3):
        part = total[6 * q : 6 * q + 6, :]
        charge.append(jnp.concatenate([part, pltpu.roll(part, 64, 1), jnp.zeros((4, 128), F32)], axis=0))
    lane = iota((16, 128), 1)

    def orbitals(side, flat):
        i = flat % BLK
        mol, a = i // 6, i % 6
        got = [jnp.take_along_axis(x, mol + MB * side, axis=1) for x in charge]
        return jnp.where(a < 4, got[0], jnp.where(a == 4, got[1], got[2]))

    def pick(f, which, values):
        place = pos_full[f][which]
        one = jnp.where(iota((16, SLOTS), 0) == place, 1.0, 0.0)
        return lax.dot_general(
            one, values, (((0,), (0,)), ((), ())), precision=lax.Precision.HIGHEST, preferred_element_type=F32
        )

    pos_full = [[s[0:1, :], s[1:2, :]] for s in (a_slots, b_slots)]
    for f in range(2):
        row_q[f] = pick(f, 0, orbitals(2 * f, lane))
        for p in range(3):
            col_q[f, p] = pick(f, 1, orbitals(2 * f + 1, lane + 128 * p))

    wide_lane = iota((SLOTS, 128), 1)

    def assemble(f, h_ref, m_ref, blk):
        def group(g, _):
            for p in range(3):
                lanes = pl.ds(pl.multiple_of((3 * g + p) * 128, 128), 128)
                h, m = h_ref[:, lanes].astype(F32), m_ref[:, lanes].astype(F32)
                i = 4 * g + (wide_lane + 128 * p) // BLK
                shift = jnp.take_along_axis(row_q[f], i, axis=1) + col_q[f, p]
                hamiltonian = h + 0.5 * m * shift
                blk[:, lanes] = (CHEM * m - hamiltonian).astype(BF16)
            return 0

        return group

    def chunk_lanes(c):
        return pl.ds(pl.multiple_of(c * LANES, 128), LANES)

    def send_r(c):
        at = chunk_lanes(c)
        return remote(blk_r.at[:, at], got_r.at[:, at], r_s.at[c], r_r.at[c], dev(n_down, w))

    def send_l(c):
        at = chunk_lanes(c)
        return remote(blk_l.at[:, at], got_l.at[:, at], l_s.at[c], l_r.at[c], dev(n, w_down))

    loads[0].wait()
    loads[1].wait()

    def make_r(c, _):
        lax.fori_loop(4 * c, 4 * c + 4, assemble(1, h_r, m_r, blk_r), 0)
        send_r(c).start()
        return 0

    lax.fori_loop(0, CHUNKS, make_r, 0)
    loads[2].wait()
    loads[3].wait()
    lax.fori_loop(0, 4 * CHUNKS, assemble(0, h_l, m_l, blk_l), 0)

    lane72 = iota((SLOTS, 128), 1)
    lane24 = iota((2 * TB, 128), 1)

    def spread(k, blk, c, compact):
        def group(q, _):
            at = pl.multiple_of(c * LANES + q * 384, 128)
            t = [blk[:, pl.ds(pl.multiple_of(at + 128 * p, 128), 128)].astype(F32) for p in range(3)]
            y0 = t[0]
            y1 = pltpu.roll(jnp.where(lane72 >= 96, t[0], t[1]), 32, 1)
            y2 = pltpu.roll(jnp.where(lane72 >= 64, t[1], t[2]), 64, 1)
            y3 = pltpu.roll(t[2], 96, 1)
            pairs = jnp.concatenate(
                [jnp.concatenate([y0, y1], axis=0), jnp.concatenate([y2, y3], axis=0)], axis=1
            ).astype(BF16)
            d = jnp.dot(sel[k], pairs, preferred_element_type=F32)
            tiles = []
            for half in range(2):
                b = [d[t * 2 * TB : (t + 1) * 2 * TB, 128 * half : 128 * half + 128] for t in range(TB)]
                if compact:
                    packed = []
                    for g in range(0, TB, 4):
                        r1, r2, r3 = (pltpu.roll(b[g + 1 + s], 96 - 32 * s, 1) for s in range(3))
                        packed += [
                            jnp.where(lane24 < 96, b[g], r1),
                            jnp.where(lane24 < 64, r1, r2),
                            jnp.where(lane24 < 32, r2, r3),
                        ]
                    b = packed
                tiles.append(b)
            at = pl.ds(pl.multiple_of(q * 4 * TB, 16), 4 * TB)
            for t, (top, low) in enumerate(zip(*tiles, strict=True)):
                rows_ir[at, 128 * t : 128 * t + 128] = jnp.concatenate([top, low], axis=0).astype(BF16)
            return 0

        lax.fori_loop(0, ROWS // 4, group, 0)

    def spread_right(k, blk, c, dst):
        spread(k, blk, c, True)
        for s in range(3):
            at = slice(384 * s, 384 * s + 384)
            ordered = jnp.dot(perm[...], rows_ir[:, at], preferred_element_type=F32).astype(BF16)
            for t in range(TB):
                to = pl.ds(pl.multiple_of(t * 128 + c * ROWS, 16), ROWS)
                right[dst, to, at] = ordered[t * ROWS : (t + 1) * ROWS]

    def spread_left(k, blk, c):
        spread(k, blk, c, False)
        for s in range(3):
            at = slice(512 * s, 512 * s + 512)
            rows_ri[:, at] = jnp.dot(perm[...], rows_ir[:, at], preferred_element_type=F32).astype(BF16)

    def own_right(c, _):
        spread_right(1, blk_r, c, 0)
        return 0

    def own_left(c, _):
        spread_left(0, blk_l, c)
        for s in range(3):
            at = slice(384 * s, 384 * s + 384)
            first[c, :, at] = jnp.dot(rows_ri[...], right[0, :, at], preferred_element_type=F32)
        return 0

    lax.fori_loop(0, CHUNKS, own_right, 0)
    lax.fori_loop(0, CHUNKS, own_left, 0)

    for copy in pos_copies:
        copy.wait_recv()
    selection(2, pos_got[0, 0:1, 0:SLOTS])
    selection(3, pos_got[1, 0:1, 0:SLOTS])

    def next_right(c, _):
        send_r(c).wait_send()
        send_l(c).start()
        send_r(c).wait_recv()
        spread_right(3, got_r, c, 1)
        return 0

    lax.fori_loop(0, CHUNKS, next_right, 0)

    def write(c):
        rows = pl.ds(pl.multiple_of(c * ROWS, 16), ROWS)
        return pltpu.make_async_copy(done.at[c], out.at[:, rows, :], out_sem.at[c])

    def next_left(c, _):
        send_l(c).wait_recv()
        spread_left(2, got_l, c)
        for s in range(3):
            at = slice(384 * s, 384 * s + 384)
            both = first[c, :, at] + jnp.dot(rows_ri[...], right[1, :, at], preferred_element_type=F32)
            both = both.astype(BF16)
            for t in range(TB):
                done[c, t, :, at] = both[t * ROWS : (t + 1) * ROWS]
        write(c).start()
        return 0

    lax.fori_loop(0, CHUNKS, next_left, 0)

    def finish(c, _):
        send_l(c).wait_send()
        write(c).wait()
        return 0

    lax.fori_loop(0, CHUNKS, finish, 0)
    for copy in asks + replies + pos_copies + [tab_copy]:
        copy.wait_send()


def local(*args):
    a_h, a_m, a_slots, a_count, a_mol, b_h, b_m, b_slots, b_count, b_mol, table = args
    anywhere = pl.BlockSpec(memory_space=pl.ANY)
    vmem = pl.BlockSpec(memory_space=pltpu.VMEM)
    dma = pltpu.SemaphoreType.DMA
    tile = pltpu.VMEM((SLOTS, FLAT), BF16)
    scratch = [tile] * 8 + [
        pltpu.VMEM((2, KPAD, SIDE), BF16),
        pltpu.VMEM((CHUNKS, PART, SIDE), F32),
        pltpu.VMEM((PART, KPAD), BF16),
        pltpu.VMEM((PART, KPAD), BF16),
        pltpu.VMEM((CHUNKS, TB, ROWS, SIDE), BF16),
        pltpu.VMEM((4, 2 * TB * TB, 2 * SLOTS), BF16),
        pltpu.VMEM((PART, PART), BF16),
        pltpu.VMEM((2, 8, 128), I32),
        pltpu.VMEM((2, 8, 128), I32),
        pltpu.VMEM((8, 128), I32),
        pltpu.VMEM((CHIPS, 8, 128), I32),
        pltpu.VMEM((CHIPS, 18, 128), F32),
        pltpu.VMEM((CHIPS, 18, 128), F32),
        pltpu.VMEM((3, TABLE), F32),
        pltpu.VMEM((6 * CHIPS, 128), I32),
        pltpu.VMEM((6 * CHIPS, 128), I32),
        pltpu.VMEM((3, 6 * CHIPS, 128), F32),
        pltpu.VMEM((2, SLOTS, 128), F32),
        pltpu.VMEM((2, 3, SLOTS, 128), F32),
        dma((4,)), dma((CHUNKS,)),
        dma((CHIPS,)), dma((CHIPS,)), dma((CHIPS,)), dma((CHIPS,)),
        dma((2,)), dma((2,)), dma(()), dma(()),
        dma((CHUNKS,)), dma((CHUNKS,)), dma((CHUNKS,)), dma((CHUNKS,)),
    ]
    result = pl.pallas_call(
        kernel,
        out_shape=jax.ShapeDtypeStruct((TB, BLK, SIDE), BF16),
        in_specs=[anywhere, anywhere, vmem, vmem, vmem, anywhere, anywhere, vmem, vmem, vmem, vmem],
        out_specs=anywhere,
        scratch_shapes=scratch,
        compiler_params=pltpu.CompilerParams(
            collective_id=0, has_side_effects=True, vmem_limit_bytes=56 * 2**20
        ),
        cost_estimate=pl.CostEstimate(flops=14 * 10**9, bytes_accessed=9 * 10**6, transcendentals=0),
    )(
        a_h[0, 0], a_m[0, 0], a_slots[0, 0], a_count, a_mol[0, 0],
        b_h[0, 0], b_m[0, 0], b_slots[0, 0], b_count, b_mol[0, 0], table,
    )
    return result.reshape(1, 1, SIDE, SIDE)


def solution(mesh):
    blocks = P("narrow", "wide", None, None)
    count = P("narrow", "wide")
    molecules = P("narrow", "wide", None, None, None)
    factor = (blocks, blocks, blocks, count, molecules)
    return jax.shard_map(
        local,
        mesh=mesh,
        in_specs=factor + factor + (P(None, "wide"),),
        out_specs=blocks,
        check_vma=False,
    )
```

```python
import functools

import jax
import jax.numpy as jnp
from jax import lax
from jax.experimental import pallas as pl
from jax.experimental.pallas import tpu as pltpu
from jax.sharding import PartitionSpec as P

TB = 12
MB = 16
BLK = 96
SLOTS = 72
FLAT = BLK * BLK
ROWS = 16
CHUNKS = BLK // ROWS
LANES = ROWS * BLK
PART = TB * ROWS
KPAD = TB * 128
SIDE = TB * BLK
CHIPS = 16
NW, NN = 32, 8
TABLE = 12288
HALF = TABLE // 128
RAW = 1
STRIPS = RAW * LANES // 128
EARLY = 6
RELAY = 2
PIECE = 8 * BLK
CHEM = 0.3

MESH = pl.DeviceIdType.MESH
F32, BF16, I32 = jnp.float32, jnp.bfloat16, jnp.int32


def iota(shape, dim):
    return lax.broadcasted_iota(I32, shape, dim)


def kernel(
    a_h, a_m, a_slots, a_count, a_mol, b_h, b_m, b_slots, b_count, b_mol, table, out,
    h_l, m_l, h_r, m_r, blk_l, blk_r, got_l, got_r, raw_h, raw_m, hop, charge_own, charge_got, right, first, rows_ir, rows_ri,
    sel, perm, pos, pos_got, ask, asked, reply, answer, summed, lines, parts, row_q, col_q,
    load_sem, ask_s, ask_r, rep_s, rep_r, pos_s, pos_r, tab_s, tab_r,
    l_s, l_r, r_s, r_r, raw_s, raw_r, chg_s, chg_r, hop_s, hop_r, leg_s, leg_r,
):
    n, w = lax.axis_index("narrow"), lax.axis_index("wide")
    core, chip = lax.rem(w, 2), lax.div(w, 2)
    partner = w + 1 - 2 * core
    beyond = lax.rem(w - 1 + 2 * core + NW, NW)
    w_down = lax.rem(w + NW - 1, NW)
    n_down, n_up = lax.rem(n + NN - 1, NN), lax.rem(n + 1, NN)

    def dev(nn, ww):
        return {"narrow": nn, "wide": ww}

    z = 2 * lax.rem(chip, 4) + lax.rem(n, 2)

    def along_z(up):
        to = lax.rem(z + up, 8)
        return n - lax.rem(n, 2) + lax.rem(to, 2), 2 * (chip - lax.rem(chip, 4) + lax.div(to, 2))

    up_n, up_w = along_z(3)
    from_n, from_w = along_z(5)
    relay = dev(up_n, up_w)
    last = dev(from_n, lax.rem(from_w + NW - 1, NW))
    home = lax.rem(chip + 1, CHIPS)
    zr = lax.rem(2 * lax.rem(home, 4) + lax.rem(n, 2) + 3, 8)
    giver = dev(n - lax.rem(n, 2) + lax.rem(zr, 2), 2 * (home - lax.rem(home, 4) + lax.div(zr, 2)))

    chip_y, chip_z = lax.div(chip, 4), lax.rem(chip, 4)

    def peer(k):
        return dev(n, 8 * lax.rem(chip_y + k // 4, 4) + 2 * lax.rem(chip_z + k % 4, 4) + core)

    def back(k):
        return (4 - k // 4) % 4 * 4 + (4 - k % 4) % 4

    loads = [
        pltpu.make_async_copy(src, dst, load_sem.at[k])
        for k, (src, dst) in enumerate([(b_h, h_r), (b_m, m_r), (a_h, h_l), (a_m, m_l)])
    ]
    for copy in loads:
        copy.start()

    barrier = pltpu.get_barrier_semaphore()
    known = [peer(i) for i in range(1, CHIPS)]
    known += [dev(n, partner), dev(n, beyond), dev(n_down, w), dev(n_up, w)]
    for device in known:
        pl.semaphore_signal(barrier, inc=1, device_id=device, device_id_type=MESH)

    @pl.when(core == 0)
    def _():
        for device in (relay, dev(from_n, from_w), last):
            pl.semaphore_signal(barrier, inc=1, device_id=device, device_id_type=MESH)

    @pl.when(core == 1)
    def _():
        pl.semaphore_signal(barrier, inc=1, device_id=giver, device_id_type=MESH)

    mols = jnp.concatenate([a_mol[:, 0, :], a_mol[:, 1, :], b_mol[:, 0, :], b_mol[:, 1, :]], axis=1)
    folded = jnp.concatenate([mols[0:6], mols[6:12]], axis=1)
    ask[0:6, :] = folded
    ask[6:8, :] = jnp.zeros((2, 128), I32)
    asked[0, 0:6, :] = folded
    for f, (slots, count) in enumerate([(a_slots, a_count), (b_slots, b_count)]):
        place = slots[1:2, :] * (2 * TB) + slots[0:1, :]
        live = iota((1, SLOTS), 1) < count[0:1, 0:1]
        pos[f] = jnp.full((8, 128), -1, I32)
        pos[f, 0:1, 0:SLOTS] = jnp.where(live, place, -1)
        pos[f, 1:3, 0:SLOTS] = slots[...]

    def line(h, _):
        for q in range(3):
            lines[q, pl.ds(h, 1), :] = table[q : q + 1, pl.ds(pl.multiple_of(h * 128, 128), 128)]
        return 0

    lax.fori_loop(0, HALF, line, 0, unroll=8)
    for q in range(3):
        top = lines[q].astype(BF16)
        parts[q * HALF : (q + 1) * HALF, 0:128] = top
        parts[q * HALF : (q + 1) * HALF, 128:256] = (lines[q] - top.astype(F32)).astype(BF16)

    pl.semaphore_wait(barrier, len(known) + 3 - 2 * core)

    def remote(src, dst, s, r, device):
        return pltpu.make_async_remote_copy(
            src_ref=src, dst_ref=dst, send_sem=s, recv_sem=r, device_id=device, device_id_type=MESH
        )

    asks = [remote(ask, asked.at[back(i)], ask_s.at[i], ask_r.at[back(i)], peer(i)) for i in range(1, CHIPS)]
    for copy in asks:
        copy.start()
    tab_copy = remote(
        parts.at[0 : 3 * HALF], parts.at[3 * HALF : 6 * HALF], tab_s, tab_r, dev(n, partner)
    )
    tab_copy.start()
    pos_copies = [
        remote(pos.at[0], pos_got.at[0], pos_s.at[0], pos_r.at[0], dev(n, w_down)),
        remote(pos.at[1], pos_got.at[1], pos_s.at[1], pos_r.at[1], dev(n_down, w)),
    ]
    for copy in pos_copies:
        copy.start()

    def chunk_lanes(c):
        return pl.ds(pl.multiple_of(c * LANES, 128), LANES)

    def strip(k):
        at = pl.ds(pl.multiple_of(k * 128, 128), 128)
        remote(b_h.at[:, at], raw_h.at[:, at], raw_s.at[0], raw_r.at[0], dev(n_down, w)).start()
        remote(b_m.at[:, at], raw_m.at[:, at], raw_s.at[1], raw_r.at[1], dev(n_down, w)).start()

    strips = slice(0, RAW * LANES)
    raws = [
        remote(b_h.at[:, strips], raw_h, raw_s.at[0], raw_r.at[0], dev(n_down, w)),
        remote(b_m.at[:, strips], raw_m, raw_s.at[1], raw_r.at[1], dev(n_down, w)),
    ]
    for k in range(EARLY):
        strip(k)

    def selection(k, place):
        wide = jnp.concatenate([place, jnp.where(place < 0, -1, place + TB)], axis=1)
        hit = iota((2 * TB * TB, 2 * SLOTS), 0) == wide
        sel[k] = jnp.where(hit, 1.0, 0.0).astype(BF16)

    selection(0, pos[0, 0:1, 0:SLOTS])
    selection(1, pos[1, 0:1, 0:SLOTS])
    pr, pc = iota((PART, PART), 0), iota((PART, PART), 1)
    perm[...] = jnp.where(pc == (pr % ROWS) * TB + pr // ROWS, 1.0, 0.0).astype(BF16)
    for k in range(2):
        for t in range(TB):
            right[k, t * 128 + BLK : (t + 1) * 128, :] = jnp.zeros((128 - BLK, SIDE), BF16)

    tab_copy.wait_recv()
    low = iota((128, 256), 0)
    high = iota((HALF, 256), 0)

    def search(k):
        ids = asked[k, 0:6, :] - chip * (2 * TABLE)
        for j in range(0, 6, 2):
            mine = jnp.concatenate([ids[j : j + 1], ids[j + 1 : j + 2]], axis=1)
            hi, lo = mine >> 7, mine & 127
            one = jnp.where(low == lo, 1.0, 0.0).astype(BF16)
            one = jnp.concatenate([one, one], axis=0)
            both = jnp.dot(parts[...], one, preferred_element_type=F32)
            in_own, in_other = high == hi - core * HALF, high == hi - (1 - core) * HALF
            for q in range(3):
                own = both[q * HALF : (q + 1) * HALF]
                other = both[(q + 3) * HALF : (q + 4) * HALF]
                hit = jnp.where(in_own, own, jnp.where(in_other, other, 0.0))
                hit = jnp.sum(hit, axis=0, keepdims=True)
                reply[k, 6 * q + j : 6 * q + j + 1, :] = hit[:, 0:128]
                reply[k, 6 * q + j + 1 : 6 * q + j + 2, :] = hit[:, 128:256]

    def serve(k, _):
        remote(ask, asked.at[k], ask_s.at[k], ask_r.at[k], peer(k)).wait_recv()
        search(k)

        @pl.when(k < 4 + STRIPS - EARLY)
        def _():
            strip(k + EARLY - 4)

        return 0

    y_copies = []
    search(0)
    for dy in range(1, 4):
        lax.fori_loop(4 * dy, 4 * dy + 4, serve, 0)
        y_copies.append(
            remote(reply.at[pl.ds(4 * dy, 4)], answer.at[4 - dy], rep_s.at[dy], rep_r.at[4 - dy], peer(4 * dy))
        )
        y_copies[-1].start()
    for k in range(1, 4):
        remote(ask, asked.at[k], ask_s.at[k], ask_r.at[k], peer(k)).wait_recv()
        search(k)
    for copy in y_copies:
        copy.wait_recv()
    for k in range(4):
        reply[k] = reply[k] + answer[1, k] + answer[2, k] + answer[3, k]
    z_copies = [
        remote(reply.at[dz], summed.at[4 - dz], rep_s.at[3 + dz], rep_r.at[7 - dz], peer(dz)) for dz in range(1, 4)
    ]
    for copy in z_copies:
        copy.start()
    for copy in z_copies:
        copy.wait_recv()
    replies = y_copies + z_copies
    total = reply[0] + summed[1] + summed[2] + summed[3]
    charge_own[...] = total
    charge_copy = remote(charge_own, charge_got, chg_s, chg_r, dev(n_down, w))
    charge_copy.start()

    lane = iota((16, 128), 1)

    def orbitals(charges, side, flat):
        i = flat % BLK
        mol, a = i // 6, i % 6
        got = []
        for q in range(3):
            part = charges[6 * q : 6 * q + 6, :]
            part = jnp.concatenate([part, pltpu.roll(part, 64, 1), jnp.zeros((4, 128), F32)], axis=0)
            got.append(jnp.take_along_axis(part, mol + MB * side, axis=1))
        return jnp.where(a < 4, got[0], jnp.where(a == 4, got[1], got[2]))

    def pick(place, values):
        one = jnp.where(iota((16, SLOTS), 0) == place, 1.0, 0.0)
        return lax.dot_general(
            one, values, (((0,), (0,)), ((), ())), precision=lax.Precision.HIGHEST, preferred_element_type=F32
        )

    def shifts(f, charges, side, row, col):
        row_q[f] = pick(row, orbitals(charges, side, lane))
        for p in range(3):
            col_q[f, p] = pick(col, orbitals(charges, side + 1, lane + 128 * p))

    shifts(1, total, 2, b_slots[0:1, :], b_slots[1:2, :])

    wide_lane = iota((SLOTS, 128), 1)

    def assemble(f, h_ref, m_ref, blk):
        def group(g, _):
            for p in range(3):
                lanes = pl.ds(pl.multiple_of((3 * g + p) * 128, 128), 128)
                h, m = h_ref[:, lanes].astype(F32), m_ref[:, lanes].astype(F32)
                i = 4 * g + (wide_lane + 128 * p) // BLK
                shift = jnp.take_along_axis(row_q[f], i, axis=1) + col_q[f, p]
                hamiltonian = h + 0.5 * m * shift
                blk[:, lanes] = (CHEM * m - hamiltonian).astype(BF16)
            return 0

        return group

    def send_r(c):
        at = chunk_lanes(c)
        return remote(blk_r.at[:, at], got_r.at[:, at], r_s.at[c], r_r.at[c], dev(n_down, w))

    def send_l(c):
        at = chunk_lanes(c)
        return remote(blk_l.at[:, at], got_l.at[:, at], l_s.at[c], l_r.at[c], dev(n, w_down))

    def piece(k):
        return slice(k * PIECE, (k + 1) * PIECE)

    def first_leg(k):
        return remote(blk_l.at[:, piece(k)], hop.at[:, piece(k)], hop_s.at[k], hop_r.at[k], relay)

    def second_leg(k):
        return remote(hop.at[:, piece(k)], got_l.at[:, piece(k)], leg_s.at[k], leg_r.at[k], last)

    def straight(k):
        return remote(blk_l.at[:, piece(k)], got_l.at[:, piece(k)], leg_s.at[k], leg_r.at[k], dev(n, w_down))

    def make_r(c, _):
        lax.fori_loop(4 * c, 4 * c + 4, assemble(1, h_r, m_r, blk_r), 0)
        send_r(c).start()
        return 0

    for copy in loads:
        copy.wait()
    make_r(RAW, 0)
    shifts(0, total, 0, a_slots[0:1, :], a_slots[1:2, :])
    lax.fori_loop(0, 4, assemble(0, h_l, m_l, blk_l), 0)

    @pl.when(core == 0)
    def _():
        for k in range(RELAY):
            first_leg(k).start()

    @pl.when(core == 1)
    def _():
        for k in range(RELAY):
            straight(k).start()

    lax.fori_loop(RAW + 1, CHUNKS, make_r, 0)
    lax.fori_loop(0, 4 * RAW, assemble(1, h_r, m_r, blk_r), 0)
    lax.fori_loop(4, 4 * CHUNKS, assemble(0, h_l, m_l, blk_l), 0)
    send_l(1).start()

    lane72 = iota((SLOTS, 128), 1)
    lane24 = iota((2 * TB, 128), 1)

    def spread(k, blk, c, compact):
        def group(q):
            at = pl.multiple_of(c * LANES + q * 384, 128)
            t = [blk[:, pl.ds(pl.multiple_of(at + 128 * p, 128), 128)].astype(F32) for p in range(3)]
            y0 = t[0]
            y1 = pltpu.roll(jnp.where(lane72 >= 96, t[0], t[1]), 32, 1)
            y2 = pltpu.roll(jnp.where(lane72 >= 64, t[1], t[2]), 64, 1)
            y3 = pltpu.roll(t[2], 96, 1)
            pairs = jnp.concatenate(
                [jnp.concatenate([y0, y1], axis=0), jnp.concatenate([y2, y3], axis=0)], axis=1
            ).astype(BF16)
            d = jnp.dot(sel[k], pairs, preferred_element_type=F32)
            tiles = []
            for half in range(2):
                b = [d[t * 2 * TB : (t + 1) * 2 * TB, 128 * half : 128 * half + 128] for t in range(TB)]
                if compact:
                    packed = []
                    for g in range(0, TB, 4):
                        r1, r2, r3 = (pltpu.roll(b[g + 1 + s], 96 - 32 * s, 1) for s in range(3))
                        packed += [
                            jnp.where(lane24 < 96, b[g], r1),
                            jnp.where(lane24 < 64, r1, r2),
                            jnp.where(lane24 < 32, r2, r3),
                        ]
                    b = packed
                tiles.append(b)
            at = slice(q * 4 * TB, (q + 1) * 4 * TB)
            for t, (top, low) in enumerate(zip(*tiles, strict=True)):
                rows_ir[at, 128 * t : 128 * t + 128] = jnp.concatenate([top, low], axis=0).astype(BF16)

        for q in range(ROWS // 4):
            group(q)

    def spread_right(k, blk, c, dst):
        spread(k, blk, c, True)
        for s in range(3):
            at = slice(384 * s, 384 * s + 384)
            ordered = jnp.dot(perm[...], rows_ir[:, at], preferred_element_type=F32).astype(BF16)
            for t in range(TB):
                to = pl.ds(pl.multiple_of(t * 128 + c * ROWS, 16), ROWS)
                right[dst, to, at] = ordered[t * ROWS : (t + 1) * ROWS]

    def spread_left(k, blk, c):
        spread(k, blk, c, False)
        for s in range(3):
            at = slice(512 * s, 512 * s + 512)
            rows_ri[:, at] = jnp.dot(perm[...], rows_ir[:, at], preferred_element_type=F32).astype(BF16)

    def own_right(c, _):
        spread_right(1, blk_r, c, 0)
        return 0

    def own_left(c, _):
        spread_left(0, blk_l, c)
        for s in range(3):
            at = slice(384 * s, 384 * s + 384)
            first[c, :, at] = jnp.dot(rows_ri[...], right[0, :, at], preferred_element_type=F32)
        return 0

    lax.fori_loop(0, CHUNKS, own_right, 0)
    send_l(2).start()
    send_l(3).start()
    lax.fori_loop(0, CHUNKS // 2, own_left, 0)

    @pl.when(core == 0)
    def _():
        for k in range(RELAY):
            first_leg(k).wait_recv()
            second_leg(k).start()

    lax.fori_loop(CHUNKS // 2, CHUNKS, own_left, 0)

    for copy in pos_copies:
        copy.wait_recv()
    selection(2, pos_got[0, 0:1, 0:SLOTS])
    selection(3, pos_got[1, 0:1, 0:SLOTS])

    send_l(4).start()
    send_l(5).start()
    charge_copy.wait_recv()
    shifts(2, charge_got[...], 2, pos_got[1, 1:2, 0:SLOTS], pos_got[1, 2:3, 0:SLOTS])
    for copy in raws:
        copy.wait_recv()
    lax.fori_loop(0, 4 * RAW, assemble(2, raw_h, raw_m, got_r), 0)

    def next_raw(c, _):
        spread_right(3, got_r, c, 1)
        return 0

    def next_right(c, _):
        send_r(c).wait_recv()
        spread_right(3, got_r, c, 1)
        return 0

    lax.fori_loop(0, RAW, next_raw, 0)
    lax.fori_loop(RAW, CHUNKS, next_right, 0)

    def finish_left(c):
        spread_left(2, got_l, c)
        rows = pl.ds(pl.multiple_of(c * ROWS, 16), ROWS)
        for s in range(3):
            at = slice(384 * s, 384 * s + 384)
            both = first[c, :, at] + jnp.dot(rows_ri[...], right[1, :, at], preferred_element_type=F32)
            both = both.astype(BF16)
            for t in range(TB):
                out[t, rows, at] = both[t * ROWS : (t + 1) * ROWS]

    def next_left(c, _):
        send_l(c).wait_recv()
        finish_left(c)
        return 0

    for copy in asks + replies + pos_copies + raws + [tab_copy, charge_copy]:
        copy.wait_send()
    lax.fori_loop(1, 3, next_left, 0)
    for k in range(RELAY):
        straight(k).wait_recv()
    finish_left(0)
    lax.fori_loop(3, CHUNKS, next_left, 0)

    def finish(c, _):
        send_l(c).wait_send()
        return 0

    lax.fori_loop(1, CHUNKS, finish, 0)
    for k in range(RELAY):
        straight(k).wait_send()

    @pl.when(core == 0)
    def _():
        for k in range(RELAY):
            first_leg(k).wait_send()

    for c in range(RAW, CHUNKS):
        send_r(c).wait_send()


def local(*args):
    a_h, a_m, a_slots, a_count, a_mol, b_h, b_m, b_slots, b_count, b_mol, table = args
    anywhere = pl.BlockSpec(memory_space=pl.ANY)
    vmem = pl.BlockSpec(memory_space=pltpu.VMEM)
    dma = pltpu.SemaphoreType.DMA
    tile = pltpu.VMEM((SLOTS, FLAT), BF16)
    raw = pltpu.VMEM((SLOTS, RAW * LANES), BF16)
    scratch = [tile] * 8 + [raw] * 2 + [
        pltpu.VMEM((SLOTS, RELAY * PIECE), BF16),
        pltpu.VMEM((18, 128), F32),
        pltpu.VMEM((18, 128), F32),
        pltpu.VMEM((2, KPAD, SIDE), BF16),
        pltpu.VMEM((CHUNKS, PART, SIDE), F32),
        pltpu.VMEM((PART, KPAD), BF16),
        pltpu.VMEM((PART, KPAD), BF16),
        pltpu.VMEM((4, 2 * TB * TB, 2 * SLOTS), BF16),
        pltpu.VMEM((PART, PART), BF16),
        pltpu.VMEM((2, 8, 128), I32),
        pltpu.VMEM((2, 8, 128), I32),
        pltpu.VMEM((8, 128), I32),
        pltpu.VMEM((CHIPS, 8, 128), I32),
        pltpu.VMEM((CHIPS, 18, 128), F32),
        pltpu.VMEM((4, 4, 18, 128), F32),
        pltpu.VMEM((4, 18, 128), F32),
        pltpu.VMEM((3, HALF, 128), F32),
        pltpu.VMEM((6 * HALF, 256), BF16),
        pltpu.VMEM((3, SLOTS, 128), F32),
        pltpu.VMEM((3, 3, SLOTS, 128), F32),
        dma((4,)),
        dma((CHIPS,)), dma((CHIPS,)), dma((CHIPS,)), dma((CHIPS,)),
        dma((2,)), dma((2,)), dma(()), dma(()),
        dma((CHUNKS,)), dma((CHUNKS,)), dma((CHUNKS,)), dma((CHUNKS,)),
        dma((2,)), dma((2,)), dma(()), dma(()),
        dma((RELAY,)), dma((RELAY,)), dma((4,)), dma((4,)),
    ]
    result = pl.pallas_call(
        kernel,
        out_shape=pltpu.VMEM((TB, BLK, SIDE), BF16),
        in_specs=[anywhere, anywhere, vmem, vmem, vmem, anywhere, anywhere, vmem, vmem, vmem, vmem],
        out_specs=vmem,
        scratch_shapes=scratch,
        compiler_params=pltpu.CompilerParams(
            collective_id=0, has_side_effects=True, vmem_limit_bytes=56 * 2**20
        ),
        cost_estimate=pl.CostEstimate(flops=14 * 10**9, bytes_accessed=9 * 10**6, transcendentals=0),
    )(
        a_h[0, 0], a_m[0, 0], a_slots[0, 0], a_count, jnp.swapaxes(a_mol[0, 0], 0, 1),
        b_h[0, 0], b_m[0, 0], b_slots[0, 0], b_count, jnp.swapaxes(b_mol[0, 0], 0, 1), table,
    )
    return result.reshape(1, 1, SIDE, SIDE)


def solution(mesh):
    blocks = P("narrow", "wide", None, None)
    count = P("narrow", "wide")
    molecules = P("narrow", "wide", None, None, None)
    factor = (blocks, blocks, blocks, count, molecules)
    return jax.shard_map(
        local,
        mesh=mesh,
        in_specs=factor + factor + (P(None, "wide"),),
        out_specs=blocks,
        check_vma=False,
    )
```

```python
import functools

import jax
import jax.numpy as jnp
from jax import lax
from jax.experimental import pallas as pl
from jax.experimental.pallas import tpu as pltpu
from jax.sharding import PartitionSpec as P

TB = 12
MB = 16
BLK = 96
SLOTS = 72
FLAT = BLK * BLK
ROWS = 16
CHUNKS = BLK // ROWS
LANES = ROWS * BLK
PART = TB * ROWS
KPAD = TB * 128
SIDE = TB * BLK
CHIPS = 16
NW, NN = 32, 8
TABLE = 12288
HALF = TABLE // 128
RAW = 24
REST = (RAW // ROWS + 1) * ROWS - RAW
FULL = (RAW + REST) // ROWS
STRIPS = RAW * BLK // 128
EARLY = 8
LATE = 4
RELAY = 2
PIECE = 8 * BLK
CHEM = 0.3

MESH = pl.DeviceIdType.MESH
F32, BF16, I32 = jnp.float32, jnp.bfloat16, jnp.int32


def iota(shape, dim):
    return lax.broadcasted_iota(I32, shape, dim)


def kernel(
    a_h, a_m, a_slots, a_count, a_mol, b_h, b_m, b_slots, b_count, b_mol, table, out,
    h_l, m_l, h_r, m_r, blk_l, blk_r, got_l, got_r, raw_h, raw_m, hop, charge_own, charge_got, right, first, rows_ir, rows_ri,
    sel, perm, pos, pos_got, ask, asked, reply, answer, summed, lines, parts, row_q, col_q,
    load_sem, ask_s, ask_r, rep_s, rep_r, pos_s, pos_r, tab_s, tab_r,
    l_s, l_r, r_s, r_r, raw_s, raw_r, chg_s, chg_r, hop_s, hop_r, leg_s, leg_r,
):
    n, w = lax.axis_index("narrow"), lax.axis_index("wide")
    core, chip = lax.rem(w, 2), lax.div(w, 2)
    partner = w + 1 - 2 * core
    beyond = lax.rem(w - 1 + 2 * core + NW, NW)
    w_down = lax.rem(w + NW - 1, NW)
    n_down, n_up = lax.rem(n + NN - 1, NN), lax.rem(n + 1, NN)

    def dev(nn, ww):
        return {"narrow": nn, "wide": ww}

    z = 2 * lax.rem(chip, 4) + lax.rem(n, 2)

    def along_z(up):
        to = lax.rem(z + up, 8)
        return n - lax.rem(n, 2) + lax.rem(to, 2), 2 * (chip - lax.rem(chip, 4) + lax.div(to, 2))

    up_n, up_w = along_z(3)
    from_n, from_w = along_z(5)
    relay = dev(up_n, up_w)
    last = dev(from_n, lax.rem(from_w + NW - 1, NW))
    home = lax.rem(chip + 1, CHIPS)
    zr = lax.rem(2 * lax.rem(home, 4) + lax.rem(n, 2) + 3, 8)
    giver = dev(n - lax.rem(n, 2) + lax.rem(zr, 2), 2 * (home - lax.rem(home, 4) + lax.div(zr, 2)))

    chip_y, chip_z = lax.div(chip, 4), lax.rem(chip, 4)

    def peer(k):
        return dev(n, 8 * lax.rem(chip_y + k // 4, 4) + 2 * lax.rem(chip_z + k % 4, 4) + core)

    def back(k):
        return (4 - k // 4) % 4 * 4 + (4 - k % 4) % 4

    loads = [
        pltpu.make_async_copy(src, dst, load_sem.at[k])
        for k, (src, dst) in enumerate([(b_h, h_r), (b_m, m_r), (a_h, h_l), (a_m, m_l)])
    ]
    for copy in loads:
        copy.start()

    barrier = pltpu.get_barrier_semaphore()
    known = [peer(i) for i in range(1, CHIPS)]
    known += [dev(n, partner), dev(n, beyond), dev(n_down, w), dev(n_up, w)]
    for device in known:
        pl.semaphore_signal(barrier, inc=1, device_id=device, device_id_type=MESH)

    @pl.when(core == 0)
    def _():
        for device in (relay, dev(from_n, from_w), last):
            pl.semaphore_signal(barrier, inc=1, device_id=device, device_id_type=MESH)

    @pl.when(core == 1)
    def _():
        pl.semaphore_signal(barrier, inc=1, device_id=giver, device_id_type=MESH)

    mols = jnp.concatenate([a_mol[:, 0, :], a_mol[:, 1, :], b_mol[:, 0, :], b_mol[:, 1, :]], axis=1)
    folded = jnp.concatenate([mols[0:6], mols[6:12]], axis=1)
    ask[0:6, :] = folded
    ask[6:8, :] = jnp.zeros((2, 128), I32)
    asked[0, 0:6, :] = folded
    for f, (slots, count) in enumerate([(a_slots, a_count), (b_slots, b_count)]):
        place = slots[1:2, :] * (2 * TB) + slots[0:1, :]
        live = iota((1, SLOTS), 1) < count[0:1, 0:1]
        pos[f] = jnp.full((8, 128), -1, I32)
        pos[f, 0:1, 0:SLOTS] = jnp.where(live, place, -1)
        pos[f, 1:3, 0:SLOTS] = slots[...]

    def line(h, _):
        for q in range(3):
            lines[q, pl.ds(h, 1), :] = table[q : q + 1, pl.ds(pl.multiple_of(h * 128, 128), 128)]
        return 0

    lax.fori_loop(0, HALF, line, 0, unroll=8)
    for q in range(3):
        top = lines[q].astype(BF16)
        parts[q * HALF : (q + 1) * HALF, 0:128] = top
        parts[q * HALF : (q + 1) * HALF, 128:256] = (lines[q] - top.astype(F32)).astype(BF16)

    pl.semaphore_wait(barrier, len(known) + 3 - 2 * core)

    def remote(src, dst, s, r, device):
        return pltpu.make_async_remote_copy(
            src_ref=src, dst_ref=dst, send_sem=s, recv_sem=r, device_id=device, device_id_type=MESH
        )

    asks = [remote(ask, asked.at[back(i)], ask_s.at[i], ask_r.at[back(i)], peer(i)) for i in range(1, CHIPS)]
    for copy in asks:
        copy.start()
    tab_copy = remote(
        parts.at[0 : 3 * HALF], parts.at[3 * HALF : 6 * HALF], tab_s, tab_r, dev(n, partner)
    )
    tab_copy.start()
    pos_copies = [
        remote(pos.at[0], pos_got.at[0], pos_s.at[0], pos_r.at[0], dev(n, w_down)),
        remote(pos.at[1], pos_got.at[1], pos_s.at[1], pos_r.at[1], dev(n_down, w)),
    ]
    for copy in pos_copies:
        copy.start()

    def chunk_lanes(c):
        return pl.ds(pl.multiple_of(c * LANES, 128), LANES)

    def strip(k):
        at = pl.ds(pl.multiple_of(k * 128, 128), 128)
        remote(b_h.at[:, at], raw_h.at[:, at], raw_s.at[0], raw_r.at[0], dev(n_down, w)).start()
        remote(b_m.at[:, at], raw_m.at[:, at], raw_s.at[1], raw_r.at[1], dev(n_down, w)).start()

    strips = slice(0, RAW * BLK)
    raws = [
        remote(b_h.at[:, strips], raw_h, raw_s.at[0], raw_r.at[0], dev(n_down, w)),
        remote(b_m.at[:, strips], raw_m, raw_s.at[1], raw_r.at[1], dev(n_down, w)),
    ]
    for k in range(EARLY):
        strip(k)

    def selection(k, place):
        wide = jnp.concatenate([place, jnp.where(place < 0, -1, place + TB)], axis=1)
        hit = iota((2 * TB * TB, 2 * SLOTS), 0) == wide
        sel[k] = jnp.where(hit, 1.0, 0.0).astype(BF16)

    selection(0, pos[0, 0:1, 0:SLOTS])
    selection(1, pos[1, 0:1, 0:SLOTS])
    pr, pc = iota((PART, PART), 0), iota((PART, PART), 1)
    perm[...] = jnp.where(pc == (pr % ROWS) * TB + pr // ROWS, 1.0, 0.0).astype(BF16)
    for k in range(2):
        for t in range(TB):
            right[k, t * 128 + BLK : (t + 1) * 128, :] = jnp.zeros((128 - BLK, SIDE), BF16)

    tab_copy.wait_recv()
    low = iota((128, 256), 0)
    line8 = iota((8, 256), 0)

    def search(k):
        ids = asked[k, 0:6, :] - chip * (2 * TABLE)
        for j in range(0, 6, 2):
            mine = jnp.concatenate([ids[j : j + 1], ids[j + 1 : j + 2]], axis=1)
            hi, lo = mine >> 7, mine & 127
            one = jnp.where(low == lo, 1.0, 0.0).astype(BF16)
            one = jnp.concatenate([one, one], axis=0)
            both = jnp.dot(parts[...], one, preferred_element_type=F32)
            hits = [jnp.zeros((8, 256), F32)] * 3
            for side, base in ((0, core * HALF), (3, (1 - core) * HALF)):
                for t in range(0, HALF, 8):
                    here = line8 == hi - (base + t)
                    for q in range(3):
                        at = (q + side) * HALF + t
                        hits[q] = jnp.where(here, both[at : at + 8], hits[q])
            for q in range(3):
                hit = jnp.sum(hits[q], axis=0, keepdims=True)
                reply[k, 6 * q + j : 6 * q + j + 1, :] = hit[:, 0:128]
                reply[k, 6 * q + j + 1 : 6 * q + j + 2, :] = hit[:, 128:256]

    def serve(k, _):
        remote(ask, asked.at[k], ask_s.at[k], ask_r.at[k], peer(k)).wait_recv()
        search(k)

        @pl.when(k < 4 + STRIPS - EARLY - LATE)
        def _():
            strip(k + EARLY - 4)

        return 0

    y_copies = []
    search(0)
    for dy in range(1, 4):
        lax.fori_loop(4 * dy, 4 * dy + 4, serve, 0)
        y_copies.append(
            remote(reply.at[pl.ds(4 * dy, 4)], answer.at[4 - dy], rep_s.at[dy], rep_r.at[4 - dy], peer(4 * dy))
        )
        y_copies[-1].start()
    for k in range(1, 4):
        remote(ask, asked.at[k], ask_s.at[k], ask_r.at[k], peer(k)).wait_recv()
        search(k)
    for copy in y_copies:
        copy.wait_recv()
    for k in range(4):
        reply[k] = reply[k] + answer[1, k] + answer[2, k] + answer[3, k]
    z_copies = [
        remote(reply.at[dz], summed.at[4 - dz], rep_s.at[3 + dz], rep_r.at[7 - dz], peer(dz)) for dz in range(1, 4)
    ]
    for copy in z_copies:
        copy.start()
    for k in range(STRIPS - LATE, STRIPS):
        strip(k)
    for copy in z_copies:
        copy.wait_recv()
    replies = y_copies + z_copies
    total = reply[0] + summed[1] + summed[2] + summed[3]
    charge_own[...] = total
    charge_copy = remote(charge_own, charge_got, chg_s, chg_r, dev(n_down, w))
    charge_copy.start()

    lane = iota((16, 128), 1)

    def orbitals(charges, side, flat):
        i = flat % BLK
        mol, a = i // 6, i % 6
        got = []
        for q in range(3):
            part = charges[6 * q : 6 * q + 6, :]
            part = jnp.concatenate([part, pltpu.roll(part, 64, 1), jnp.zeros((4, 128), F32)], axis=0)
            got.append(jnp.take_along_axis(part, mol + MB * side, axis=1))
        return jnp.where(a < 4, got[0], jnp.where(a == 4, got[1], got[2]))

    def pick(place, values):
        one = jnp.where(iota((16, SLOTS), 0) == place, 1.0, 0.0)
        return lax.dot_general(
            one, values, (((0,), (0,)), ((), ())), precision=lax.Precision.HIGHEST, preferred_element_type=F32
        )

    def shifts(f, charges, side, row, col):
        row_q[f] = pick(row, orbitals(charges, side, lane))
        for p in range(3):
            col_q[f, p] = pick(col, orbitals(charges, side + 1, lane + 128 * p))

    shifts(1, total, 2, b_slots[0:1, :], b_slots[1:2, :])

    wide_lane = iota((SLOTS, 128), 1)

    def assemble(f, h_ref, m_ref, blk):
        def group(g, _):
            for p in range(3):
                lanes = pl.ds(pl.multiple_of((3 * g + p) * 128, 128), 128)
                h, m = h_ref[:, lanes].astype(F32), m_ref[:, lanes].astype(F32)
                i = 4 * g + (wide_lane + 128 * p) // BLK
                shift = jnp.take_along_axis(row_q[f], i, axis=1) + col_q[f, p]
                hamiltonian = h + 0.5 * m * shift
                blk[:, lanes] = (CHEM * m - hamiltonian).astype(BF16)
            return 0

        return group

    def send_r(c):
        at = chunk_lanes(c)
        return remote(blk_r.at[:, at], got_r.at[:, at], r_s.at[c], r_r.at[c], dev(n_down, w))

    def send_l(c):
        at = chunk_lanes(c)
        return remote(blk_l.at[:, at], got_l.at[:, at], l_s.at[c], l_r.at[c], dev(n, w_down))

    def piece(k):
        return slice(k * PIECE, (k + 1) * PIECE)

    def first_leg(k):
        return remote(blk_l.at[:, piece(k)], hop.at[:, piece(k)], hop_s.at[k], hop_r.at[k], relay)

    def second_leg(k):
        return remote(hop.at[:, piece(k)], got_l.at[:, piece(k)], leg_s.at[k], leg_r.at[k], last)

    def straight(k):
        return remote(blk_l.at[:, piece(k)], got_l.at[:, piece(k)], leg_s.at[k], leg_r.at[k], dev(n, w_down))

    rest_at = slice(RAW * BLK, (RAW + REST) * BLK)
    rest = remote(blk_r.at[:, rest_at], got_r.at[:, rest_at], r_s.at[0], r_r.at[0], dev(n_down, w))

    def make_r(c, _):
        lax.fori_loop(4 * c, 4 * c + 4, assemble(1, h_r, m_r, blk_r), 0)
        send_r(c).start()
        return 0

    for copy in loads:
        copy.wait()
    lax.fori_loop(RAW // 4, (RAW + REST) // 4, assemble(1, h_r, m_r, blk_r), 0)
    rest.start()
    shifts(0, total, 0, a_slots[0:1, :], a_slots[1:2, :])
    lax.fori_loop(0, 4, assemble(0, h_l, m_l, blk_l), 0)

    @pl.when(core == 0)
    def _():
        for k in range(RELAY):
            first_leg(k).start()

    @pl.when(core == 1)
    def _():
        for k in range(RELAY):
            straight(k).start()

    lax.fori_loop(FULL, CHUNKS, make_r, 0)
    lax.fori_loop(0, RAW // 4, assemble(1, h_r, m_r, blk_r), 0)
    lax.fori_loop(4, 4 * CHUNKS, assemble(0, h_l, m_l, blk_l), 0)
    send_l(1).start()

    lane72 = iota((SLOTS, 128), 1)
    lane24 = iota((2 * TB, 128), 1)

    def spread(k, blk, c, compact):
        def group(q):
            at = pl.multiple_of(c * LANES + q * 384, 128)
            t = [blk[:, pl.ds(pl.multiple_of(at + 128 * p, 128), 128)].astype(F32) for p in range(3)]
            y0 = t[0]
            y1 = pltpu.roll(jnp.where(lane72 >= 96, t[0], t[1]), 32, 1)
            y2 = pltpu.roll(jnp.where(lane72 >= 64, t[1], t[2]), 64, 1)
            y3 = pltpu.roll(t[2], 96, 1)
            pairs = jnp.concatenate(
                [jnp.concatenate([y0, y1], axis=0), jnp.concatenate([y2, y3], axis=0)], axis=1
            ).astype(BF16)
            d = jnp.dot(sel[k], pairs, preferred_element_type=F32)
            tiles = []
            for half in range(2):
                b = [d[t * 2 * TB : (t + 1) * 2 * TB, 128 * half : 128 * half + 128] for t in range(TB)]
                if compact:
                    packed = []
                    for g in range(0, TB, 4):
                        r1, r2, r3 = (pltpu.roll(b[g + 1 + s], 96 - 32 * s, 1) for s in range(3))
                        packed += [
                            jnp.where(lane24 < 96, b[g], r1),
                            jnp.where(lane24 < 64, r1, r2),
                            jnp.where(lane24 < 32, r2, r3),
                        ]
                    b = packed
                tiles.append(b)
            at = slice(q * 4 * TB, (q + 1) * 4 * TB)
            for t, (top, low) in enumerate(zip(*tiles, strict=True)):
                rows_ir[at, 128 * t : 128 * t + 128] = jnp.concatenate([top, low], axis=0).astype(BF16)

        for q in range(ROWS // 4):
            group(q)

    def spread_right(k, blk, c, dst):
        spread(k, blk, c, True)
        for s in range(3):
            at = slice(384 * s, 384 * s + 384)
            ordered = jnp.dot(perm[...], rows_ir[:, at], preferred_element_type=F32).astype(BF16)
            for t in range(TB):
                to = pl.ds(pl.multiple_of(t * 128 + c * ROWS, 16), ROWS)
                right[dst, to, at] = ordered[t * ROWS : (t + 1) * ROWS]

    def spread_left(k, blk, c):
        spread(k, blk, c, False)
        for s in range(3):
            at = slice(512 * s, 512 * s + 512)
            rows_ri[:, at] = jnp.dot(perm[...], rows_ir[:, at], preferred_element_type=F32).astype(BF16)

    def own_right(c, _):
        spread_right(1, blk_r, c, 0)
        return 0

    def own_left(c, _):
        spread_left(0, blk_l, c)
        for s in range(3):
            at = slice(384 * s, 384 * s + 384)
            first[c, :, at] = jnp.dot(rows_ri[...], right[0, :, at], preferred_element_type=F32)
        return 0

    lax.fori_loop(0, CHUNKS, own_right, 0)
    send_l(2).start()
    send_l(3).start()
    lax.fori_loop(0, CHUNKS // 2, own_left, 0)

    @pl.when(core == 0)
    def _():
        for k in range(RELAY):
            first_leg(k).wait_recv()
            second_leg(k).start()

    lax.fori_loop(CHUNKS // 2, CHUNKS, own_left, 0)

    for copy in pos_copies:
        copy.wait_recv()
    selection(2, pos_got[0, 0:1, 0:SLOTS])
    selection(3, pos_got[1, 0:1, 0:SLOTS])

    send_l(4).start()
    send_l(5).start()
    charge_copy.wait_recv()
    shifts(2, charge_got[...], 2, pos_got[1, 1:2, 0:SLOTS], pos_got[1, 2:3, 0:SLOTS])
    for copy in raws:
        copy.wait_recv()
    lax.fori_loop(0, RAW // 4, assemble(2, raw_h, raw_m, got_r), 0)
    rest.wait_recv()

    def next_raw(c, _):
        spread_right(3, got_r, c, 1)
        return 0

    def next_right(c, _):
        send_r(c).wait_recv()
        spread_right(3, got_r, c, 1)
        return 0

    lax.fori_loop(0, FULL, next_raw, 0)
    lax.fori_loop(FULL, CHUNKS, next_right, 0)

    def finish_left(c):
        spread_left(2, got_l, c)
        rows = pl.ds(pl.multiple_of(c * ROWS, 16), ROWS)
        for s in range(3):
            at = slice(384 * s, 384 * s + 384)
            both = first[c, :, at] + jnp.dot(rows_ri[...], right[1, :, at], preferred_element_type=F32)
            both = both.astype(BF16)
            for t in range(TB):
                out[t, rows, at] = both[t * ROWS : (t + 1) * ROWS]

    def next_left(c, _):
        send_l(c).wait_recv()
        finish_left(c)
        return 0

    for copy in asks + replies + pos_copies + raws + [tab_copy, charge_copy]:
        copy.wait_send()
    lax.fori_loop(1, 3, next_left, 0)
    for k in range(RELAY):
        straight(k).wait_recv()
    finish_left(0)
    lax.fori_loop(3, CHUNKS, next_left, 0)

    def finish(c, _):
        send_l(c).wait_send()
        return 0

    lax.fori_loop(1, CHUNKS, finish, 0)
    for k in range(RELAY):
        straight(k).wait_send()

    @pl.when(core == 0)
    def _():
        for k in range(RELAY):
            first_leg(k).wait_send()

    rest.wait_send()
    for c in range(FULL, CHUNKS):
        send_r(c).wait_send()


def local(*args):
    a_h, a_m, a_slots, a_count, a_mol, b_h, b_m, b_slots, b_count, b_mol, table = args
    anywhere = pl.BlockSpec(memory_space=pl.ANY)
    vmem = pl.BlockSpec(memory_space=pltpu.VMEM)
    dma = pltpu.SemaphoreType.DMA
    tile = pltpu.VMEM((SLOTS, FLAT), BF16)
    raw = pltpu.VMEM((SLOTS, RAW * BLK), BF16)
    scratch = [tile] * 8 + [raw] * 2 + [
        pltpu.VMEM((SLOTS, RELAY * PIECE), BF16),
        pltpu.VMEM((18, 128), F32),
        pltpu.VMEM((18, 128), F32),
        pltpu.VMEM((2, KPAD, SIDE), BF16),
        pltpu.VMEM((CHUNKS, PART, SIDE), F32),
        pltpu.VMEM((PART, KPAD), BF16),
        pltpu.VMEM((PART, KPAD), BF16),
        pltpu.VMEM((4, 2 * TB * TB, 2 * SLOTS), BF16),
        pltpu.VMEM((PART, PART), BF16),
        pltpu.VMEM((2, 8, 128), I32),
        pltpu.VMEM((2, 8, 128), I32),
        pltpu.VMEM((8, 128), I32),
        pltpu.VMEM((CHIPS, 8, 128), I32),
        pltpu.VMEM((CHIPS, 18, 128), F32),
        pltpu.VMEM((4, 4, 18, 128), F32),
        pltpu.VMEM((4, 18, 128), F32),
        pltpu.VMEM((3, HALF, 128), F32),
        pltpu.VMEM((6 * HALF, 256), BF16),
        pltpu.VMEM((3, SLOTS, 128), F32),
        pltpu.VMEM((3, 3, SLOTS, 128), F32),
        dma((4,)),
        dma((CHIPS,)), dma((CHIPS,)), dma((CHIPS,)), dma((CHIPS,)),
        dma((2,)), dma((2,)), dma(()), dma(()),
        dma((CHUNKS,)), dma((CHUNKS,)), dma((CHUNKS,)), dma((CHUNKS,)),
        dma((2,)), dma((2,)), dma(()), dma(()),
        dma((RELAY,)), dma((RELAY,)), dma((4,)), dma((4,)),
    ]
    result = pl.pallas_call(
        kernel,
        out_shape=pltpu.VMEM((TB, BLK, SIDE), BF16),
        in_specs=[anywhere, anywhere, vmem, vmem, vmem, anywhere, anywhere, vmem, vmem, vmem, vmem],
        out_specs=vmem,
        scratch_shapes=scratch,
        compiler_params=pltpu.CompilerParams(
            collective_id=0, has_side_effects=True, vmem_limit_bytes=56 * 2**20
        ),
        cost_estimate=pl.CostEstimate(flops=14 * 10**9, bytes_accessed=9 * 10**6, transcendentals=0),
    )(
        a_h[0, 0], a_m[0, 0], a_slots[0, 0], a_count, jnp.swapaxes(a_mol[0, 0], 0, 1),
        b_h[0, 0], b_m[0, 0], b_slots[0, 0], b_count, jnp.swapaxes(b_mol[0, 0], 0, 1), table,
    )
    return result.reshape(1, 1, SIDE, SIDE)


def solution(mesh):
    blocks = P("narrow", "wide", None, None)
    count = P("narrow", "wide")
    molecules = P("narrow", "wide", None, None, None)
    factor = (blocks, blocks, blocks, count, molecules)
    return jax.shard_map(
        local,
        mesh=mesh,
        in_specs=factor + factor + (P(None, "wide"),),
        out_specs=blocks,
        check_vma=False,
    )
```

```python
import functools

import jax
import jax.numpy as jnp
from jax import lax
from jax.experimental import pallas as pl
from jax.experimental.pallas import tpu as pltpu
from jax.sharding import PartitionSpec as P

TB = 12
MB = 16
BLK = 96
SLOTS = 72
FLAT = BLK * BLK
ROWS = 16
CHUNKS = BLK // ROWS
LANES = ROWS * BLK
PART = TB * ROWS
KPAD = TB * 128
SIDE = TB * BLK
CHIPS = 16
NW, NN = 32, 8
TABLE = 12288
HALF = TABLE // 128
RAW = 20
REST = (RAW // ROWS + 1) * ROWS - RAW
FULL = (RAW + REST) // ROWS
STRIPS = RAW * BLK // 128
EARLY = 9
LATE = 4
RELAY = 2
PIECE = 8 * BLK
CHEM = 0.3

MESH = pl.DeviceIdType.MESH
F32, BF16, I32 = jnp.float32, jnp.bfloat16, jnp.int32


def iota(shape, dim):
    return lax.broadcasted_iota(I32, shape, dim)


def kernel(
    a_h, a_m, a_slots, a_count, a_mol, b_h, b_m, b_slots, b_count, b_mol, table, out,
    h_l, m_l, h_r, m_r, blk_l, blk_r, got_l, got_r, raw_h, raw_m, hop, charge_own, charge_got, right, first, rows_ir, rows_ri,
    sel, perm, pos, pos_got, ask, asked, reply, answer, summed, lines, parts, row_q, col_q,
    load_sem, ask_s, ask_r, rep_s, rep_r, pos_s, pos_r, tab_s, tab_r,
    l_s, l_r, r_s, r_r, raw_s, raw_r, chg_s, chg_r, hop_s, hop_r, leg_s, leg_r,
):
    n, w = lax.axis_index("narrow"), lax.axis_index("wide")
    core, chip = lax.rem(w, 2), lax.div(w, 2)
    partner = w + 1 - 2 * core
    beyond = lax.rem(w - 1 + 2 * core + NW, NW)
    w_down = lax.rem(w + NW - 1, NW)
    n_down, n_up = lax.rem(n + NN - 1, NN), lax.rem(n + 1, NN)

    def dev(nn, ww):
        return {"narrow": nn, "wide": ww}

    z = 2 * lax.rem(chip, 4) + lax.rem(n, 2)

    def along_z(up):
        to = lax.rem(z + up, 8)
        return n - lax.rem(n, 2) + lax.rem(to, 2), 2 * (chip - lax.rem(chip, 4) + lax.div(to, 2))

    up_n, up_w = along_z(3)
    from_n, from_w = along_z(5)
    relay = dev(up_n, up_w)
    last = dev(from_n, lax.rem(from_w + NW - 1, NW))
    home = lax.rem(chip + 1, CHIPS)
    zr = lax.rem(2 * lax.rem(home, 4) + lax.rem(n, 2) + 3, 8)
    giver = dev(n - lax.rem(n, 2) + lax.rem(zr, 2), 2 * (home - lax.rem(home, 4) + lax.div(zr, 2)))

    chip_y, chip_z = lax.div(chip, 4), lax.rem(chip, 4)

    def peer(k):
        return dev(n, 8 * lax.rem(chip_y + k // 4, 4) + 2 * lax.rem(chip_z + k % 4, 4) + core)

    def back(k):
        return (4 - k // 4) % 4 * 4 + (4 - k % 4) % 4

    loads = [
        pltpu.make_async_copy(src, dst, load_sem.at[k])
        for k, (src, dst) in enumerate([(b_h, h_r), (b_m, m_r), (a_h, h_l), (a_m, m_l)])
    ]
    for copy in loads:
        copy.start()

    barrier = pltpu.get_barrier_semaphore()
    known = [peer(i) for i in range(1, CHIPS)]
    known += [dev(n, partner), dev(n, beyond), dev(n_down, w), dev(n_up, w)]
    for device in known:
        pl.semaphore_signal(barrier, inc=1, device_id=device, device_id_type=MESH)

    @pl.when(core == 0)
    def _():
        for device in (relay, dev(from_n, from_w), last):
            pl.semaphore_signal(barrier, inc=1, device_id=device, device_id_type=MESH)

    @pl.when(core == 1)
    def _():
        pl.semaphore_signal(barrier, inc=1, device_id=giver, device_id_type=MESH)

    for at, mol in ((0, b_mol), (3, a_mol)):
        mols = jnp.concatenate([mol[:, 0, :], mol[:, 1, :]], axis=1)
        folded = jnp.concatenate([mols[3 * g : 3 * g + 3] for g in range(4)], axis=1)
        ask[at : at + 3, :] = folded
        asked[0, at : at + 3, :] = folded
    ask[6:8, :] = jnp.zeros((2, 128), I32)
    for f, (slots, count) in enumerate([(a_slots, a_count), (b_slots, b_count)]):
        place = slots[1:2, :] * (2 * TB) + slots[0:1, :]
        live = iota((1, SLOTS), 1) < count[0:1, 0:1]
        pos[f] = jnp.full((8, 128), -1, I32)
        pos[f, 0:1, 0:SLOTS] = jnp.where(live, place, -1)
        pos[f, 1:3, 0:SLOTS] = slots[...]

    def line(h, _):
        for q in range(3):
            lines[q, pl.ds(h, 1), :] = table[q : q + 1, pl.ds(pl.multiple_of(h * 128, 128), 128)]
        return 0

    lax.fori_loop(0, HALF, line, 0, unroll=8)
    for q in range(3):
        top = lines[q].astype(BF16)
        parts[q * HALF : (q + 1) * HALF, 0:128] = top
        parts[q * HALF : (q + 1) * HALF, 128:256] = (lines[q] - top.astype(F32)).astype(BF16)

    pl.semaphore_wait(barrier, len(known) + 3 - 2 * core)

    def remote(src, dst, s, r, device):
        return pltpu.make_async_remote_copy(
            src_ref=src, dst_ref=dst, send_sem=s, recv_sem=r, device_id=device, device_id_type=MESH
        )

    asks = [remote(ask, asked.at[back(i)], ask_s, ask_r.at[back(i)], peer(i)) for i in range(1, CHIPS)]
    all_asks = remote(asked.at[pl.ds(1, CHIPS - 1)], asked.at[pl.ds(1, CHIPS - 1)], ask_s, ask_r.at[0], peer(1))
    for copy in asks:
        copy.start()
    tab_copy = remote(
        parts.at[0 : 3 * HALF], parts.at[3 * HALF : 6 * HALF], tab_s, tab_r, dev(n, partner)
    )
    tab_copy.start()
    pos_copies = [
        remote(pos.at[0], pos_got.at[0], pos_s.at[0], pos_r.at[0], dev(n, w_down)),
        remote(pos.at[1], pos_got.at[1], pos_s.at[1], pos_r.at[1], dev(n_down, w)),
    ]
    for copy in pos_copies:
        copy.start()

    def chunk_lanes(c):
        return pl.ds(pl.multiple_of(c * LANES, 128), LANES)

    def strip(k):
        at = pl.ds(pl.multiple_of(k * 128, 128), 128)
        remote(b_h.at[:, at], raw_h.at[:, at], raw_s.at[0], raw_r.at[0], dev(n_down, w)).start()
        remote(b_m.at[:, at], raw_m.at[:, at], raw_s.at[1], raw_r.at[1], dev(n_down, w)).start()

    strips = slice(0, RAW * BLK)
    raws = [
        remote(b_h.at[:, strips], raw_h, raw_s.at[0], raw_r.at[0], dev(n_down, w)),
        remote(b_m.at[:, strips], raw_m, raw_s.at[1], raw_r.at[1], dev(n_down, w)),
    ]
    for k in range(EARLY):
        strip(k)

    def selection(k, place):
        wide = jnp.concatenate([place, jnp.where(place < 0, -1, place + TB)], axis=1)
        hit = iota((2 * TB * TB, 2 * SLOTS), 0) == wide
        sel[k] = jnp.where(hit, 1.0, 0.0).astype(BF16)

    selection(0, pos[0, 0:1, 0:SLOTS])
    selection(1, pos[1, 0:1, 0:SLOTS])
    pr, pc = iota((PART, PART), 0), iota((PART, PART), 1)
    perm[...] = jnp.where(pc == (pr % ROWS) * TB + pr // ROWS, 1.0, 0.0).astype(BF16)
    for k in range(2):
        for t in range(TB):
            right[k, t * 128 + BLK : (t + 1) * 128, :] = jnp.zeros((128 - BLK, SIDE), BF16)

    tab_copy.wait_recv()
    low = iota((128, 256), 0)
    line8 = iota((8, 256), 0)

    def search(half, k):
        rows = slice(3 * half, 3 * half + 3)
        ids = jnp.concatenate([asked[k, rows, :], asked[k + 1, rows, :]], axis=0) - chip * (2 * TABLE)
        for j in range(0, 6, 2):
            mine = jnp.concatenate([ids[j : j + 1], ids[j + 1 : j + 2]], axis=1)
            hi, lo = mine >> 7, mine & 127
            one = jnp.where(low == lo, 1.0, 0.0).astype(BF16)
            one = jnp.concatenate([one, one], axis=0)
            both = jnp.dot(parts[...], one, preferred_element_type=F32)
            hits = [jnp.zeros((8, 256), F32)] * 3
            for side, base in ((0, core * HALF), (3, (1 - core) * HALF)):
                for t in range(0, HALF, 8):
                    here = line8 == hi - (base + t)
                    for q in range(3):
                        at = (q + side) * HALF + t
                        hits[q] = jnp.where(here, both[at : at + 8], hits[q])
            for q in range(3):
                hit = jnp.sum(hits[q], axis=0, keepdims=True)
                for i in range(2):
                    to = 3 * q + (j + i) % 3
                    reply[half, k + (j + i) // 3, to : to + 1, :] = hit[:, 128 * i : 128 * i + 128]

    def asked_by(k):
        remote(ask, asked.at[k], ask_s, ask_r.at[k], peer(k)).wait_recv()

    def serve(t, _):
        k = 2 * t
        asked_by(k)
        asked_by(k + 1)
        search(0, k)

        @pl.when(t < 2 + STRIPS - EARLY - LATE)
        def _():
            strip(t + EARLY - 2)

        return 0

    def serve_a(t, _):
        search(1, 2 * t)
        return 0

    def send_y(half, dy):
        copy = remote(
            reply.at[half, pl.ds(4 * dy, 4)], answer.at[half, 4 - dy],
            rep_s.at[7 * half + dy], rep_r.at[7 * half + 4 - dy], peer(4 * dy),
        )
        copy.start()
        return copy

    def send_z(half, y_copies):
        for copy in y_copies:
            copy.wait_recv()
        for k in range(4):
            reply[half, k] = reply[half, k] + answer[half, 1, k] + answer[half, 2, k] + answer[half, 3, k]
        copies = [
            remote(
                reply.at[half, dz], summed.at[half, 4 - dz],
                rep_s.at[7 * half + 3 + dz], rep_r.at[7 * half + 7 - dz], peer(dz),
            )
            for dz in range(1, 4)
        ]
        for copy in copies:
            copy.start()
        return copies

    def charges_of(half, z_copies):
        for copy in z_copies:
            copy.wait_recv()
        return reply[half, 0] + summed[half, 1] + summed[half, 2] + summed[half, 3]

    y_b, y_a = [], []
    for dy in range(1, 4):
        lax.fori_loop(2 * dy, 2 * dy + 2, serve, 0)
        y_b.append(send_y(0, dy))
    for k in range(1, 4):
        asked_by(k)
    search(0, 0)
    search(0, 2)
    for dy in range(1, 3):
        lax.fori_loop(2 * dy, 2 * dy + 2, serve_a, 0)
        y_a.append(send_y(1, dy))
    z_b = send_z(0, y_b)
    for k in range(STRIPS - LATE, STRIPS):
        strip(k)
    lax.fori_loop(6, 8, serve_a, 0)
    y_a.append(send_y(1, 3))
    lax.fori_loop(0, 2, serve_a, 0)
    z_a = send_z(1, y_a)
    replies = y_b + y_a + z_b + z_a
    total_b = charges_of(0, z_b)
    charge_own[...] = total_b
    charge_copy = remote(charge_own, charge_got, chg_s, chg_r, dev(n_down, w))
    charge_copy.start()

    lane = iota((16, 128), 1)

    def orbitals(charges, side, flat):
        i = flat % BLK
        mol, a = i // 6, i % 6
        got = []
        for q in range(3):
            part = charges[3 * q : 3 * q + 3, :]
            turned = [pltpu.roll(part, 128 - 32 * g, 1) for g in range(1, 4)]
            part = jnp.concatenate([part, *turned, jnp.zeros((4, 128), F32)], axis=0)
            got.append(jnp.take_along_axis(part, mol + MB * side, axis=1))
        return jnp.where(a < 4, got[0], jnp.where(a == 4, got[1], got[2]))

    def pick(place, values):
        one = jnp.where(iota((16, SLOTS), 0) == place, 1.0, 0.0)
        return lax.dot_general(
            one, values, (((0,), (0,)), ((), ())), precision=lax.Precision.HIGHEST, preferred_element_type=F32
        )

    def shifts(f, charges, row, col):
        row_q[f] = pick(row, orbitals(charges, 0, lane))
        for p in range(3):
            col_q[f, p] = pick(col, orbitals(charges, 1, lane + 128 * p))

    shifts(1, total_b, b_slots[0:1, :], b_slots[1:2, :])

    wide_lane = iota((SLOTS, 128), 1)

    def assemble(f, h_ref, m_ref, blk):
        def group(g, _):
            for p in range(3):
                lanes = pl.ds(pl.multiple_of((3 * g + p) * 128, 128), 128)
                h, m = h_ref[:, lanes].astype(F32), m_ref[:, lanes].astype(F32)
                i = 4 * g + (wide_lane + 128 * p) // BLK
                shift = jnp.take_along_axis(row_q[f], i, axis=1) + col_q[f, p]
                hamiltonian = h + 0.5 * m * shift
                blk[:, lanes] = (CHEM * m - hamiltonian).astype(BF16)
            return 0

        return group

    def send_r(c):
        at = chunk_lanes(c)
        return remote(blk_r.at[:, at], got_r.at[:, at], r_s.at[c], r_r.at[c], dev(n_down, w))

    def send_l(c):
        at = chunk_lanes(c)
        return remote(blk_l.at[:, at], got_l.at[:, at], l_s.at[c], l_r.at[c], dev(n, w_down))

    def piece(k):
        return slice(k * PIECE, (k + 1) * PIECE)

    def first_leg(k):
        return remote(blk_l.at[:, piece(k)], hop.at[:, piece(k)], hop_s.at[k], hop_r.at[k], relay)

    def second_leg(k):
        return remote(hop.at[:, piece(k)], got_l.at[:, piece(k)], leg_s.at[k], leg_r.at[k], last)

    def straight(k):
        return remote(blk_l.at[:, piece(k)], got_l.at[:, piece(k)], leg_s.at[k], leg_r.at[k], dev(n, w_down))

    rest_at = slice(RAW * BLK, (RAW + REST) * BLK)
    rest = remote(blk_r.at[:, rest_at], got_r.at[:, rest_at], r_s.at[0], r_r.at[0], dev(n_down, w))

    def make_r(c, _):
        lax.fori_loop(4 * c, 4 * c + 4, assemble(1, h_r, m_r, blk_r), 0)
        send_r(c).start()
        return 0

    for copy in loads:
        copy.wait()
    lax.fori_loop(RAW // 4, (RAW + REST) // 4, assemble(1, h_r, m_r, blk_r), 0)
    rest.start()
    make_r(FULL, 0)
    shifts(0, charges_of(1, z_a), a_slots[0:1, :], a_slots[1:2, :])
    lax.fori_loop(0, 4, assemble(0, h_l, m_l, blk_l), 0)

    @pl.when(core == 0)
    def _():
        for k in range(RELAY):
            first_leg(k).start()

    @pl.when(core == 1)
    def _():
        for k in range(RELAY):
            straight(k).start()

    lax.fori_loop(FULL + 1, CHUNKS, make_r, 0)
    lax.fori_loop(0, RAW // 4, assemble(1, h_r, m_r, blk_r), 0)
    lax.fori_loop(4, 4 * CHUNKS, assemble(0, h_l, m_l, blk_l), 0)
    send_l(1).start()

    lane72 = iota((SLOTS, 128), 1)
    lane24 = iota((2 * TB, 128), 1)

    def spread(k, blk, c, compact):
        def group(q):
            at = pl.multiple_of(c * LANES + q * 384, 128)
            t = [blk[:, pl.ds(pl.multiple_of(at + 128 * p, 128), 128)].astype(F32) for p in range(3)]
            y0 = t[0]
            y1 = pltpu.roll(jnp.where(lane72 >= 96, t[0], t[1]), 32, 1)
            y2 = pltpu.roll(jnp.where(lane72 >= 64, t[1], t[2]), 64, 1)
            y3 = pltpu.roll(t[2], 96, 1)
            pairs = jnp.concatenate(
                [jnp.concatenate([y0, y1], axis=0), jnp.concatenate([y2, y3], axis=0)], axis=1
            ).astype(BF16)
            d = jnp.dot(sel[k], pairs, preferred_element_type=F32)
            tiles = []
            for half in range(2):
                b = [d[t * 2 * TB : (t + 1) * 2 * TB, 128 * half : 128 * half + 128] for t in range(TB)]
                if compact:
                    packed = []
                    for g in range(0, TB, 4):
                        r1, r2, r3 = (pltpu.roll(b[g + 1 + s], 96 - 32 * s, 1) for s in range(3))
                        packed += [
                            jnp.where(lane24 < 96, b[g], r1),
                            jnp.where(lane24 < 64, r1, r2),
                            jnp.where(lane24 < 32, r2, r3),
                        ]
                    b = packed
                tiles.append(b)
            at = slice(q * 4 * TB, (q + 1) * 4 * TB)
            for t, (top, low) in enumerate(zip(*tiles, strict=True)):
                rows_ir[at, 128 * t : 128 * t + 128] = jnp.concatenate([top, low], axis=0).astype(BF16)

        for q in range(ROWS // 4):
            group(q)

    def spread_right(k, blk, c, dst):
        spread(k, blk, c, True)
        for s in range(3):
            at = slice(384 * s, 384 * s + 384)
            ordered = jnp.dot(perm[...], rows_ir[:, at], preferred_element_type=F32).astype(BF16)
            for t in range(TB):
                to = pl.ds(pl.multiple_of(t * 128 + c * ROWS, 16), ROWS)
                right[dst, to, at] = ordered[t * ROWS : (t + 1) * ROWS]

    def spread_left(k, blk, c):
        spread(k, blk, c, False)
        for s in range(3):
            at = slice(512 * s, 512 * s + 512)
            rows_ri[:, at] = jnp.dot(perm[...], rows_ir[:, at], preferred_element_type=F32).astype(BF16)

    def own_right(c, _):
        spread_right(1, blk_r, c, 0)
        return 0

    def own_left(c, _):
        spread_left(0, blk_l, c)
        for s in range(3):
            at = slice(384 * s, 384 * s + 384)
            first[c, :, at] = jnp.dot(rows_ri[...], right[0, :, at], preferred_element_type=F32)
        return 0

    lax.fori_loop(0, CHUNKS, own_right, 0)
    send_l(2).start()
    send_l(3).start()
    lax.fori_loop(0, CHUNKS // 2, own_left, 0)

    @pl.when(core == 0)
    def _():
        for k in range(RELAY):
            first_leg(k).wait_recv()
            second_leg(k).start()

    lax.fori_loop(CHUNKS // 2, CHUNKS, own_left, 0)

    for copy in pos_copies:
        copy.wait_recv()
    selection(2, pos_got[0, 0:1, 0:SLOTS])
    selection(3, pos_got[1, 0:1, 0:SLOTS])

    send_l(4).start()
    send_l(5).start()
    charge_copy.wait_recv()
    shifts(2, charge_got[...], pos_got[1, 1:2, 0:SLOTS], pos_got[1, 2:3, 0:SLOTS])
    for copy in raws:
        copy.wait_recv()
    lax.fori_loop(0, RAW // 4, assemble(2, raw_h, raw_m, got_r), 0)
    rest.wait_recv()

    def next_raw(c, _):
        spread_right(3, got_r, c, 1)
        return 0

    def next_right(c, _):
        send_r(c).wait_recv()
        spread_right(3, got_r, c, 1)
        return 0

    lax.fori_loop(0, FULL, next_raw, 0)
    lax.fori_loop(FULL, CHUNKS, next_right, 0)

    def finish_left(c):
        spread_left(2, got_l, c)
        rows = pl.ds(pl.multiple_of(c * ROWS, 16), ROWS)
        for s in range(3):
            at = slice(384 * s, 384 * s + 384)
            both = first[c, :, at] + jnp.dot(rows_ri[...], right[1, :, at], preferred_element_type=F32)
            both = both.astype(BF16)
            for t in range(TB):
                out[t, rows, at] = both[t * ROWS : (t + 1) * ROWS]

    def next_left(c, _):
        send_l(c).wait_recv()
        finish_left(c)
        return 0

    for copy in [all_asks] + replies + pos_copies + raws + [tab_copy, charge_copy]:
        copy.wait_send()
    lax.fori_loop(1, 3, next_left, 0)
    for k in range(RELAY):
        straight(k).wait_recv()
    finish_left(0)
    lax.fori_loop(3, CHUNKS, next_left, 0)

    def finish(c, _):
        send_l(c).wait_send()
        return 0

    lax.fori_loop(1, CHUNKS, finish, 0)
    for k in range(RELAY):
        straight(k).wait_send()

    @pl.when(core == 0)
    def _():
        for k in range(RELAY):
            first_leg(k).wait_send()

    rest.wait_send()
    for c in range(FULL, CHUNKS):
        send_r(c).wait_send()


def local(*args):
    a_h, a_m, a_slots, a_count, a_mol, b_h, b_m, b_slots, b_count, b_mol, table = args
    anywhere = pl.BlockSpec(memory_space=pl.ANY)
    vmem = pl.BlockSpec(memory_space=pltpu.VMEM)
    dma = pltpu.SemaphoreType.DMA
    tile = pltpu.VMEM((SLOTS, FLAT), BF16)
    raw = pltpu.VMEM((SLOTS, RAW * BLK), BF16)
    scratch = [tile] * 8 + [raw] * 2 + [
        pltpu.VMEM((SLOTS, RELAY * PIECE), BF16),
        pltpu.VMEM((9, 128), F32),
        pltpu.VMEM((9, 128), F32),
        pltpu.VMEM((2, KPAD, SIDE), BF16),
        pltpu.VMEM((CHUNKS, PART, SIDE), F32),
        pltpu.VMEM((PART, KPAD), BF16),
        pltpu.VMEM((PART, KPAD), BF16),
        pltpu.VMEM((4, 2 * TB * TB, 2 * SLOTS), BF16),
        pltpu.VMEM((PART, PART), BF16),
        pltpu.VMEM((2, 8, 128), I32),
        pltpu.VMEM((2, 8, 128), I32),
        pltpu.VMEM((8, 128), I32),
        pltpu.VMEM((CHIPS, 8, 128), I32),
        pltpu.VMEM((2, CHIPS, 9, 128), F32),
        pltpu.VMEM((2, 4, 4, 9, 128), F32),
        pltpu.VMEM((2, 4, 9, 128), F32),
        pltpu.VMEM((3, HALF, 128), F32),
        pltpu.VMEM((6 * HALF, 256), BF16),
        pltpu.VMEM((3, SLOTS, 128), F32),
        pltpu.VMEM((3, 3, SLOTS, 128), F32),
        dma((4,)),
        dma(()), dma((CHIPS,)), dma((14,)), dma((14,)),
        dma((2,)), dma((2,)), dma(()), dma(()),
        dma((CHUNKS,)), dma((CHUNKS,)), dma((CHUNKS,)), dma((CHUNKS,)),
        dma((2,)), dma((2,)), dma(()), dma(()),
        dma((RELAY,)), dma((RELAY,)), dma((4,)), dma((4,)),
    ]
    result = pl.pallas_call(
        kernel,
        out_shape=pltpu.VMEM((TB, BLK, SIDE), BF16),
        in_specs=[anywhere, anywhere, vmem, vmem, vmem, anywhere, anywhere, vmem, vmem, vmem, vmem],
        out_specs=vmem,
        scratch_shapes=scratch,
        compiler_params=pltpu.CompilerParams(
            collective_id=0, has_side_effects=True, vmem_limit_bytes=56 * 2**20
        ),
        cost_estimate=pl.CostEstimate(flops=14 * 10**9, bytes_accessed=9 * 10**6, transcendentals=0),
    )(
        a_h[0, 0], a_m[0, 0], a_slots[0, 0], a_count, jnp.swapaxes(a_mol[0, 0], 0, 1),
        b_h[0, 0], b_m[0, 0], b_slots[0, 0], b_count, jnp.swapaxes(b_mol[0, 0], 0, 1), table,
    )
    return result.reshape(1, 1, SIDE, SIDE)


def solution(mesh):
    blocks = P("narrow", "wide", None, None)
    count = P("narrow", "wide")
    molecules = P("narrow", "wide", None, None, None)
    factor = (blocks, blocks, blocks, count, molecules)
    return jax.shard_map(
        local,
        mesh=mesh,
        in_specs=factor + factor + (P(None, "wide"),),
        out_specs=blocks,
        check_vma=False,
    )
```
